32 devices in a mesh: groups: 2 (over y), dp: 4 (over z), mp: 2 (over x), seq: 2 (over core).
Axes of the slice: x: 2, y: 2, z: 4, core: 2. Of those that a mesh axis runs over, the one named last changes fastest.
Arguments:
- hidden: bfloat16 [32, 128, 14336], P(('groups', 'dp', 'seq'), None, 'mp'), parts along dimension 0, may hold values from -6 to 6
- down_weight: bfloat16 [14336, 4096], P('mp', 'dp'), may hold values from -0.046875 to 0.046875
- residual: bfloat16 [32, 128, 4096], P(('groups', 'dp', 'seq'), None, 'mp'), parts along dimension 0
- norm_gain: float32 [4096], P('mp'), may hold values from 0.5 to 1.5
- lengths: int32 [32], P(('groups', 'dp', 'seq')), parts along dimension 0, may hold values from 16 to 128
- queries: bfloat16 [8, 4096], P(('groups', 'dp'), 'mp'), parts along dimension 0
- positive_ids: int32 [8], P(('groups', 'dp')), parts along dimension 0, may hold values from 0 to 15
- negative_ids: int32 [8, 31], P(('groups', 'dp')), parts along dimension 0, may hold values from 0 to 15, as said below
- rerank_scores: int32 [8, 32], P(('groups', 'dp')), parts along dimension 0, may hold values from -64 to 63
Outputs:
- normed: bfloat16 [32, 128, 4096], P(('groups', 'dp', 'seq'), None, 'mp'), parts along dimension 0
- similarity_matrix: float32 [8, 32], P(('groups', 'dp')), parts along dimension 0
- losses: float32 [8], P(('groups', 'dp')), parts along dimension 0
The draws below stay inside these ranges and needn't reach their ends.
There are 2 independent parts, one for each index of `groups`. The reference program is written for one: setup_inputs(seed, part) draws one part's arguments, and reference() takes and returns one part's arrays. A program takes and returns all parts, laid end to end along the dimension named above; an argument that names none is the same for every part. Nothing has to cross between parts.
Inputs may be any that keep to these rules, and one draw needn't show every extreme that they name: `negative_ids`: no hard negative of a query lies among the 4 passages with the query's own index of dp; the query with index q has dp index q, and the passage with index p has dp index p // 4.
All inputs are finite; a program needn't handle non-finite values.
Results may differ from the reference program's by a relative error of at most 0.001.
Values may be sent and summed in bfloat16 or wider, within the bound.
A program may use at most 192 MiB of HBM per device.

```python
import jax
import jax.numpy as jnp
from jax import lax

D = 4096
FF = 14336
L = 128
NEG = 31
Q_DEV = 1
P_GRP = 4
PASS = 16
QUERIES = 4
CANDS = 32


def draw_residual(key, part):
    key = jax.random.fold_in(key, 11)
    column = jnp.arange(D, dtype=jnp.float32) / D
    value_rows = jax.random.normal(key, (PASS, L, D), jnp.float32)
    return (value_rows * 0.6 * jnp.power(3.0, column)).astype(jnp.bfloat16)


def draw_queries(key, part):
    key = jax.random.fold_in(key, 23)
    column = jnp.arange(D, dtype=jnp.float32) / D
    value_rows = jax.random.normal(key, (QUERIES, D), jnp.float32)
    return (value_rows * jnp.power(3.0, column)).astype(jnp.bfloat16)


def draw_negative_ids(key, part):
    key = jax.random.fold_in(key, 37)
    first_key, second_key = jax.random.split(key)
    span = PASS - P_GRP
    first = jax.random.randint(first_key, (QUERIES, NEG), 0, span)
    second = jax.random.randint(second_key, (QUERIES, NEG), 0, span)
    offset = jnp.minimum(first, second)
    block = jnp.arange(QUERIES, dtype=jnp.int32) // Q_DEV
    return ((block[:, None] * P_GRP + P_GRP + offset) % PASS).astype(jnp.int32)


def touch_ends(result, key, low, high):
    longest = result.shape.index(max(result.shape))
    spots = []
    for shift in (0, 1):
        where = [jax.random.randint(jax.random.fold_in(key, axis), (), 0, length) for axis, length in enumerate(result.shape)]
        where[longest] = (where[longest] + shift) % result.shape[longest]
        spots.append(tuple(where))
    return result.at[spots[0]].set(low).at[spots[1]].set(high)


def block_levels(own_key, extent, pieces, smallest, largest):
    def one(dim, blocks):
        heights = jax.random.uniform(jax.random.fold_in(jax.random.fold_in(own_key, 6), dim), (blocks,), jnp.float32, smallest / len(pieces), largest / len(pieces))
        return jnp.repeat(jnp.exp(heights), extent[dim] // blocks).reshape((-1,) + (1,) * (len(extent) - dim - 1))

    loudness = one(*pieces[0])
    for cut in pieces[1:]:
        loudness = loudness * one(*cut)
    return loudness


def gaussian(stream_key, dims, spread, limit, pieces=(), held_as=jnp.bfloat16):
    array = jax.random.normal(stream_key, dims, jnp.float32) * spread
    if len(pieces) > 0:
        array = block_levels(stream_key, dims, pieces, -0.22, 0.18) * array
    return jnp.clip(array, min=-limit, max=limit).astype(held_as)


def setup_inputs(seed: int = 0, part: int = 0) -> dict:
    key_list = jax.random.split(jax.random.key(seed), 10)
    part_keys = jax.random.split(jax.random.fold_in(key_list[9], part), 10)
    return {
        "hidden": gaussian(part_keys[0], (PASS, L, FF), 1.0, 6.0, ((0, 8), (2, 2))),
        "down_weight": gaussian(key_list[1], (FF, D), FF ** -0.5, 0.046875, ((0, 2), (1, 4))),
        "residual": draw_residual(jax.random.fold_in(jax.random.fold_in(key_list[9], part), 71), part),
        "norm_gain": jnp.clip(1.0 + 0.1 * jax.random.normal(key_list[3], (D,), jnp.float32), 0.5, 1.5),
        "lengths": touch_ends(jax.random.randint(part_keys[4], (PASS,), L // 8, L + 1), jax.random.fold_in(part_keys[4], 1), L // 8, L).astype(jnp.int32),
        "queries": draw_queries(jax.random.fold_in(jax.random.fold_in(key_list[9], part), 71), part),
        "positive_ids": touch_ends(jax.random.randint(part_keys[6], (QUERIES,), 0, PASS), jax.random.fold_in(part_keys[6], 1), 0, PASS - 1).astype(jnp.int32),
        "negative_ids": draw_negative_ids(jax.random.fold_in(jax.random.fold_in(key_list[9], part), 71), part),
        "rerank_scores": touch_ends(jax.random.randint(part_keys[8], (QUERIES, CANDS), -64, 64), jax.random.fold_in(part_keys[8], 1), -64, 63).astype(jnp.int32),
    }


epsilon = 1e-05
safety_margin = 1e-06
sharpness_divisor = 0.05
teacher_scale = 8.0

def partition_logarithm(value_rows):
    return jnp.log(lax.optimization_barrier(jnp.sum(jnp.exp(value_rows), axis=-1, keepdims=True)))

def reference(hidden, down_weight, residual, norm_gain, lengths, queries, positive_ids, negative_ids, rerank_scores):

    def single_passage(items):
        rows, stream = items
        branch = jnp.dot(rows, down_weight, preferred_element_type=jnp.float32)
        updated = stream.astype(jnp.float32) + branch
        squares = lax.optimization_barrier(jnp.mean(updated * updated, axis=-1))
        return updated * lax.rsqrt(squares + epsilon)[:, None] * norm_gain[None, :]
    scaled = lax.map(single_passage, (hidden, residual))
    position = jnp.arange(L, dtype=jnp.int32)
    valid_mask = position[None, :] < lengths[:, None]
    averaged_embedding = lax.optimization_barrier(jnp.sum(jnp.where(valid_mask[:, :, None], scaled, 0.0), axis=1)) / lengths.astype(jnp.float32)[:, None]
    candidates = jnp.concatenate([positive_ids[:, None], negative_ids], axis=1)
    one_hot = (candidates[:, :, None] == jnp.arange(PASS, dtype=jnp.int32)[None, None, :]).astype(jnp.float32)
    picked = jnp.einsum('qcp,pd->qcd', one_hot, averaged_embedding, precision=lax.Precision.HIGHEST)
    query_vals = queries.astype(jnp.float32)
    cosine_numerator = jnp.einsum('qd,qcd->qc', query_vals, picked, precision=lax.Precision.HIGHEST)
    candidate_length_power = lax.optimization_barrier(jnp.sum(picked * picked, axis=-1))
    question_length_power = lax.optimization_barrier(jnp.sum(query_vals * query_vals, axis=-1))
    similarity_matrix = cosine_numerator * lax.rsqrt(question_length_power + safety_margin)[:, None] * lax.rsqrt(candidate_length_power + safety_margin) / sharpness_divisor
    log_student = similarity_matrix - partition_logarithm(similarity_matrix)
    teacher = rerank_scores.astype(jnp.float32) / teacher_scale
    teacher_log_probs = teacher - partition_logarithm(teacher)
    losses = -log_student[:, 0] + lax.optimization_barrier(jnp.sum(jnp.exp(teacher_log_probs) * (teacher_log_probs - log_student), axis=-1))
    return (scaled.astype(jnp.bfloat16), similarity_matrix, losses)
```

```python
import functools

import jax
import jax.numpy as jnp
from jax import lax
from jax.experimental import pallas as pl
from jax.experimental.pallas import tpu as pltpu
from jax.sharding import PartitionSpec as P

D = 4096


epsilon = 1e-05
safety_margin = 1e-06
sharpness_divisor = 0.05
teacher_scale = 8.0


def partition_logarithm(value_rows):
    return jnp.log(jnp.sum(jnp.exp(value_rows), axis=-1, keepdims=True))


MESH = pl.DeviceIdType.MESH
CHUNKS = 7
RIGHT, LEFT, ACROSS, CORE, CORE_ACROSS = range(5)


def gather_kernel(n, w_ref, o_ref, own_sem, send, recv):
    z = lax.axis_index("dp")
    y = lax.axis_index("groups")
    c = lax.axis_index("seq")
    depth, cols = w_ref.shape
    quarter = depth // 4
    size = quarter // CHUNKS
    mine = y * 2 + c
    other = (1 - y) * 2 + c
    to = {
        RIGHT: {"dp": jnp.minimum(z + 1, n - 1)},
        LEFT: {"dp": jnp.maximum(z - 1, 0)},
        ACROSS: {"groups": 1 - y},
        CORE: {"seq": 1 - c},
        CORE_ACROSS: {"seq": 1 - c},
    }

    barrier = pltpu.get_barrier_semaphore()
    pl.semaphore_signal(barrier, inc=1, device_id=to[ACROSS], device_id_type=MESH)
    pl.semaphore_signal(barrier, inc=1, device_id=to[CORE], device_id_type=MESH)

    @pl.when(z < n - 1)
    def _():
        pl.semaphore_signal(barrier, inc=1, device_id=to[RIGHT], device_id_type=MESH)

    @pl.when(z > 0)
    def _():
        pl.semaphore_signal(barrier, inc=1, device_id=to[LEFT], device_id_type=MESH)

    own_cols = pl.ds(pl.multiple_of(z * cols, 128), cols)
    own = pltpu.make_async_copy(w_ref, o_ref.at[:, own_cols], own_sem)
    own.start()
    peers = 2 + (z < n - 1).astype(jnp.int32) + (z > 0).astype(jnp.int32)
    pl.semaphore_wait(barrier, peers)

    def rows(q, k):
        return pl.ds(pl.multiple_of(q * quarter + k * size, 16), size)

    def copy(kind, b, q, k, own_source=False):
        place = o_ref.at[rows(q, k), pl.ds(pl.multiple_of(b * cols, 128), cols)]
        return pltpu.make_async_remote_copy(
            src_ref=w_ref.at[rows(q, k), :] if own_source else place,
            dst_ref=place,
            send_sem=send.at[kind, b, k],
            recv_sem=recv.at[kind, b, k],
            device_id=to[kind],
            device_id_type=MESH,
        )

    def exists(sign, j):
        b = z + sign * j
        return jnp.logical_and(b >= 0, b < n)

    def stream(kind, sign, t):
        j, k = t // CHUNKS, t % CHUNKS
        b = z + sign * j
        goes_on = (z < n - 1) if kind == RIGHT else (z > 0)

        @pl.when(jnp.logical_and(j == 0, goes_on))
        def _():
            copy(kind, z, mine, k, own_source=True).start()

        @pl.when(jnp.logical_and(jnp.logical_and(j >= 1, j < n), exists(sign, j)))
        def _():
            copy(kind, b, mine, k).wait_recv()

            @pl.when(goes_on)
            def _():
                copy(kind, b, mine, k).start()

            copy(ACROSS, b, mine, k).start()
            copy(CORE, b, mine, k).start()

        before = t - 2
        jb, kb = before // CHUNKS, before % CHUNKS

        @pl.when(jnp.logical_and(jnp.logical_and(before >= 0, goes_on), exists(sign, jb)))
        def _():
            copy(kind, z + sign * jb, mine, kb).wait_send()

    def crossed(sign, t):
        j, k = t // CHUNKS, t % CHUNKS
        b = z + sign * j

        @pl.when(jnp.logical_and(jnp.logical_and(j >= 1, j < n), exists(sign, j)))
        def _():
            copy(ACROSS, b, other, k).wait_recv()
            copy(CORE_ACROSS, b, other, k).start()

    def step(t, carry):
        stream(RIGHT, -1, t)
        stream(LEFT, 1, t)
        crossed(-1, t - 1)
        crossed(1, t - 1)
        return carry

    lax.fori_loop(0, n * CHUNKS + 2, step, 0)

    def drain(t, carry):
        b, k = t // CHUNKS, t % CHUNKS

        @pl.when(b != z)
        def _():
            copy(ACROSS, b, mine, k).wait_send()
            copy(CORE, b, mine, k).wait()
            copy(CORE_ACROSS, b, other, k).wait()

        return carry

    lax.fori_loop(0, n * CHUNKS, drain, 0)
    own.wait()


def gather_weight(n, weight):
    depth, cols = weight.shape
    return pl.pallas_call(
        functools.partial(gather_kernel, n),
        out_shape=jax.ShapeDtypeStruct((depth, n * cols), weight.dtype),
        in_specs=[pl.BlockSpec(memory_space=pl.ANY)],
        out_specs=pl.BlockSpec(memory_space=pl.ANY),
        scratch_shapes=[
            pltpu.SemaphoreType.DMA,
            pltpu.SemaphoreType.DMA((5, n, CHUNKS)),
            pltpu.SemaphoreType.DMA((5, n, CHUNKS)),
        ],
        compiler_params=pltpu.CompilerParams(collective_id=0, has_side_effects=True),
        cost_estimate=pl.CostEstimate(
            flops=0, bytes_accessed=4 * n * depth * cols, transcendentals=0
        ),
    )(weight)


def local(
    n,
    hidden,
    down_weight,
    residual,
    norm_gain,
    lengths,
    queries,
    positive_ids,
    negative_ids,
    rerank_scores,
):
    passages, tok_len, hidden_width = hidden.shape
    flattened = hidden.reshape(passages * tok_len, hidden_width)
    partial_sum = jnp.dot(
        flattened,
        gather_weight(n, down_weight),
        preferred_element_type=jnp.float32,
    )
    partial_sum = partial_sum.reshape(passages, tok_len, D)
    branch_sum = lax.psum_scatter(partial_sum, "mp", scatter_dimension=2, tiled=True)
    updated = residual.astype(jnp.float32) + branch_sum
    squares = lax.psum(jnp.sum(updated * updated, axis=-1), "mp")
    unit_rows = updated * lax.rsqrt(squares / D + epsilon)[:, :, None]
    scaled = unit_rows * norm_gain[None, None, :]
    position = jnp.arange(tok_len, dtype=jnp.int32)
    valid_mask = position[None, :] < lengths[:, None]
    pooled_share = (
        jnp.sum(jnp.where(valid_mask[:, :, None], scaled, 0.0), axis=1)
        / lengths.astype(jnp.float32)[:, None]
    )
    averaged_embedding = lax.all_gather(pooled_share, ("dp", "seq"), axis=0, tiled=True)
    total_passages = averaged_embedding.shape[0]
    candidates = jnp.concatenate([positive_ids[:, None], negative_ids], axis=1)
    one_hot = (
        candidates[:, :, None] == jnp.arange(total_passages, dtype=jnp.int32)[None, None, :]
    ).astype(jnp.float32)
    picked = jnp.einsum("qcp,pd->qcd", one_hot, averaged_embedding, precision=lax.Precision.HIGHEST)
    query_vals = queries.astype(jnp.float32)
    cosine_numerator = jnp.einsum("qd,qcd->qc", query_vals, picked, precision=lax.Precision.HIGHEST)
    candidate_length_power = jnp.sum(picked * picked, axis=-1)
    question_length_power = jnp.sum(query_vals * query_vals, axis=-1)
    cosine_numerator, candidate_length_power, question_length_power = lax.psum(
        (cosine_numerator, candidate_length_power, question_length_power), "mp"
    )
    similarity_matrix = (
        cosine_numerator
        * lax.rsqrt(question_length_power + safety_margin)[:, None]
        * lax.rsqrt(candidate_length_power + safety_margin)
        / sharpness_divisor
    )
    log_student = similarity_matrix - partition_logarithm(similarity_matrix)
    teacher = rerank_scores.astype(jnp.float32) / teacher_scale
    teacher_log_probs = teacher - partition_logarithm(teacher)
    losses = -log_student[:, 0] + jnp.sum(
        jnp.exp(teacher_log_probs) * (teacher_log_probs - log_student), axis=-1
    )
    return (scaled.astype(jnp.bfloat16), similarity_matrix, losses)


def solution(mesh):
    return jax.shard_map(
        functools.partial(local, mesh.shape["dp"]),
        mesh=mesh,
        in_specs=(
            P(("groups", "dp", "seq"), None, "mp"),
            P("mp", "dp"),
            P(("groups", "dp", "seq"), None, "mp"),
            P("mp"),
            P(("groups", "dp", "seq")),
            P(("groups", "dp"), "mp"),
            P(("groups", "dp")),
            P(("groups", "dp"), None),
            P(("groups", "dp"), None),
        ),
        out_specs=(
            P(("groups", "dp", "seq"), None, "mp"),
            P(("groups", "dp"), None),
            P(("groups", "dp")),
        ),
        check_vma=False,
    )
```

```python
import functools

import jax
import jax.numpy as jnp
from jax import lax
from jax.experimental import pallas as pl
from jax.experimental.pallas import tpu as pltpu
from jax.sharding import PartitionSpec as P

D = 4096


epsilon = 1e-05
safety_margin = 1e-06
sharpness_divisor = 0.05
teacher_scale = 8.0


def partition_logarithm(value_rows):
    return jnp.log(jnp.sum(jnp.exp(value_rows), axis=-1, keepdims=True))


MESH = pl.DeviceIdType.MESH
CHUNKS = 14
WINDOW = 3
LAG = 2
RIGHT, LEFT, ACROSS, CORE, CORE_ACROSS = range(5)


def both(*terms):
    return functools.reduce(jnp.logical_and, terms)


def gather_kernel(w_ref, h_ref, o_ref, p_ref, t_ref, own_sem, h_send, h_recv, send, recv):
    z = lax.axis_index("dp")
    y = lax.axis_index("groups")
    c = lax.axis_index("seq")
    depth = w_ref.shape[0]
    quarter = depth // 4
    size = quarter // CHUNKS
    mine = y * 2 + c
    other = (1 - y) * 2 + c
    pair = z + 1 - 2 * (z % 2)
    to = {
        RIGHT: {"dp": jnp.minimum(z + 1, 3)},
        LEFT: {"dp": jnp.maximum(z - 1, 0)},
        ACROSS: {"groups": 1 - y},
        CORE: {"seq": 1 - c},
        CORE_ACROSS: {"seq": 1 - c},
    }

    barrier = pltpu.get_barrier_semaphore()
    pl.semaphore_signal(barrier, inc=1, device_id=to[ACROSS], device_id_type=MESH)
    pl.semaphore_signal(barrier, inc=1, device_id=to[CORE], device_id_type=MESH)

    @pl.when(z < 3)
    def _():
        pl.semaphore_signal(barrier, inc=1, device_id=to[RIGHT], device_id_type=MESH)

    @pl.when(z > 0)
    def _():
        pl.semaphore_signal(barrier, inc=1, device_id=to[LEFT], device_id_type=MESH)

    peers = 2 + (z < 3).astype(jnp.int32) + (z > 0).astype(jnp.int32)
    pl.semaphore_wait(barrier, peers)

    def rows(q, k):
        return pl.ds(pl.multiple_of(q * quarter + k * size, 16), size)

    def part(k):
        return pl.ds(pl.multiple_of(k * size, 16), size)

    def remote(kind, j, k, src, dst, arrives):
        return pltpu.make_async_remote_copy(
            src_ref=src,
            dst_ref=dst,
            send_sem=send.at[kind, j, k],
            recv_sem=recv.at[kind, arrives, k],
            device_id=to[kind],
            device_id_type=MESH,
        )

    def along(kind, j, k):
        return remote(kind, j, k, p_ref.at[part(k), :], p_ref.at[part(k), :], j)

    def shared(kind, j, k, q):
        block = jnp.where(z >= 2, z - j, z + j) % 2
        place = o_ref.at[block, rows(q, k), :]
        return remote(kind, j, k, place, place, j)

    def stream(kind, t):
        u = z if kind == RIGHT else 3 - z
        sign = -1 if kind == RIGHT else 1
        j, k = t // CHUNKS, t % CHUNKS
        own = w_ref.at[rows(mine, k), :]
        passing = p_ref.at[part(k), :]

        @pl.when(both(j == 0, u == 0))
        def _():
            remote(kind, 0, k, own, passing, 1).start()

        @pl.when(both(j == 0, u >= 1, u <= 2))
        def _():
            remote(kind, 0, k, own, o_ref.at[z % 2, rows(mine, k), :], 1).start()

        @pl.when(both(j == 1, u == 1))
        def _():
            along(kind, 1, k).wait_recv()
            place = o_ref.at[(z + sign) % 2, rows(mine, k), :]
            remote(kind, 1, k, passing, place, 2).start()

        @pl.when(jnp.logical_or(both(j == 1, u >= 2), both(j == 2, u == 2)))
        def _():
            along(kind, j, k).wait_recv()
            shared(ACROSS, j, k, mine).start()
            shared(CORE, j, k, mine).start()

        before = t - WINDOW
        jb, kb = before // CHUNKS, before % CHUNKS
        sent = jnp.logical_or(both(jb == 0, u <= 2), both(jb == 1, u == 1))

        @pl.when(both(before >= 0, sent))
        def _():
            along(kind, jb, kb).wait_send()

    def needed(j):
        return jnp.logical_or(j == 1, both(j == 2, z >= 1, z <= 2))

    swap = pltpu.make_async_remote_copy(
        src_ref=h_ref,
        dst_ref=t_ref,
        send_sem=h_send,
        recv_sem=h_recv,
        device_id={"dp": pair},
        device_id_type=MESH,
    )
    outer = jnp.logical_or(z == 0, z == 3)
    keep = pltpu.make_async_copy(w_ref, o_ref.at[z % 2], own_sem)

    def step(t, carry):
        stream(RIGHT, t)
        stream(LEFT, t)
        late = t - LAG
        j, k = late // CHUNKS, late % CHUNKS

        @pl.when(both(late >= 0, needed(j)))
        def _():
            shared(ACROSS, j, k, other).wait_recv()
            shared(CORE_ACROSS, j, k, other).start()

        @pl.when(t == CHUNKS)
        def _():
            swap.start()

            @pl.when(outer)
            def _():
                keep.start()

        return carry

    lax.fori_loop(0, 3 * CHUNKS + max(WINDOW, LAG), step, 0)

    def drain(t, carry):
        j, k = t // CHUNKS, t % CHUNKS

        @pl.when(needed(j))
        def _():
            shared(ACROSS, j, k, mine).wait_send()
            shared(CORE, j, k, mine).wait_send()
            shared(CORE, j, k, y * 2 + 1 - c).wait_recv()
            shared(CORE_ACROSS, j, k, other).wait_send()
            shared(CORE_ACROSS, j, k, (1 - y) * 2 + 1 - c).wait_recv()

        return carry

    lax.fori_loop(CHUNKS, 3 * CHUNKS, drain, 0)
    swap.wait()

    @pl.when(outer)
    def _():
        keep.wait()


def gather(weight, rows):
    depth, cols = weight.shape
    return pl.pallas_call(
        gather_kernel,
        out_shape=(
            jax.ShapeDtypeStruct((2, depth, cols), weight.dtype),
            jax.ShapeDtypeStruct((depth // 4, cols), weight.dtype),
            jax.ShapeDtypeStruct(rows.shape, rows.dtype),
        ),
        in_specs=[pl.BlockSpec(memory_space=pl.ANY)] * 2,
        out_specs=(pl.BlockSpec(memory_space=pl.ANY),) * 3,
        scratch_shapes=[
            pltpu.SemaphoreType.DMA,
            pltpu.SemaphoreType.DMA,
            pltpu.SemaphoreType.DMA,
            pltpu.SemaphoreType.DMA((5, 3, CHUNKS)),
            pltpu.SemaphoreType.DMA((5, 3, CHUNKS)),
        ],
        compiler_params=pltpu.CompilerParams(collective_id=0, has_side_effects=True),
        cost_estimate=pl.CostEstimate(
            flops=0, bytes_accessed=16 * depth * cols, transcendentals=0
        ),
    )(weight, rows)


def paired_branch(flattened, weight):
    blocks, _, theirs = gather(weight, flattened)
    half = lax.axis_index("dp") % 2
    kept_here = half == lax.axis_index("mp")
    swap_pair = [(z, z + 1 - 2 * (z % 2)) for z in range(4)]
    sums = []
    back = []
    for s in range(2):
        away = jnp.dot(theirs, blocks[s], preferred_element_type=jnp.float32)
        back.append(lax.ppermute(away, "dp", swap_pair))
    for s in range(2):
        own = jnp.dot(flattened, blocks[s], preferred_element_type=jnp.float32)
        leaves = jnp.where(kept_here, back[s], own)
        stays = jnp.where(kept_here, own, back[s])
        sums.append(stays + lax.ppermute(leaves, "mp", [(0, 1), (1, 0)]))
    return jnp.concatenate(sums, axis=1)


def local(
    paired,
    hidden,
    down_weight,
    residual,
    norm_gain,
    lengths,
    queries,
    positive_ids,
    negative_ids,
    rerank_scores,
):
    passages, tok_len, hidden_width = hidden.shape
    flattened = hidden.reshape(passages * tok_len, hidden_width)
    if paired:
        branch_sum = paired_branch(flattened, down_weight).reshape(residual.shape)
    else:
        partial_sum = jnp.dot(
            flattened,
            lax.all_gather(down_weight, "dp", axis=1, tiled=True),
            preferred_element_type=jnp.float32,
        )
        partial_sum = partial_sum.reshape(passages, tok_len, D)
        branch_sum = lax.psum_scatter(partial_sum, "mp", scatter_dimension=2, tiled=True)
    updated = residual.astype(jnp.float32) + branch_sum
    squares = lax.psum(jnp.sum(updated * updated, axis=-1), "mp")
    unit_rows = updated * lax.rsqrt(squares / D + epsilon)[:, :, None]
    scaled = unit_rows * norm_gain[None, None, :]
    position = jnp.arange(tok_len, dtype=jnp.int32)
    valid_mask = position[None, :] < lengths[:, None]
    pooled_share = (
        jnp.sum(jnp.where(valid_mask[:, :, None], scaled, 0.0), axis=1)
        / lengths.astype(jnp.float32)[:, None]
    )
    averaged_embedding = lax.all_gather(pooled_share, ("dp", "seq"), axis=0, tiled=True)
    total_passages = averaged_embedding.shape[0]
    candidates = jnp.concatenate([positive_ids[:, None], negative_ids], axis=1)
    one_hot = (
        candidates[:, :, None] == jnp.arange(total_passages, dtype=jnp.int32)[None, None, :]
    ).astype(jnp.float32)
    picked = jnp.einsum("qcp,pd->qcd", one_hot, averaged_embedding, precision=lax.Precision.HIGHEST)
    query_vals = queries.astype(jnp.float32)
    cosine_numerator = jnp.einsum("qd,qcd->qc", query_vals, picked, precision=lax.Precision.HIGHEST)
    candidate_length_power = jnp.sum(picked * picked, axis=-1)
    question_length_power = jnp.sum(query_vals * query_vals, axis=-1)
    cosine_numerator, candidate_length_power, question_length_power = lax.psum(
        (cosine_numerator, candidate_length_power, question_length_power), "mp"
    )
    similarity_matrix = (
        cosine_numerator
        * lax.rsqrt(question_length_power + safety_margin)[:, None]
        * lax.rsqrt(candidate_length_power + safety_margin)
        / sharpness_divisor
    )
    log_student = similarity_matrix - partition_logarithm(similarity_matrix)
    teacher = rerank_scores.astype(jnp.float32) / teacher_scale
    teacher_log_probs = teacher - partition_logarithm(teacher)
    losses = -log_student[:, 0] + jnp.sum(
        jnp.exp(teacher_log_probs) * (teacher_log_probs - log_student), axis=-1
    )
    return (scaled.astype(jnp.bfloat16), similarity_matrix, losses)


def solution(mesh):
    paired = (mesh.shape["dp"], mesh.shape["mp"]) == (4, 2)
    paired = paired and (mesh.shape["groups"], mesh.shape["seq"]) == (2, 2)
    return jax.shard_map(
        functools.partial(local, paired),
        mesh=mesh,
        in_specs=(
            P(("groups", "dp", "seq"), None, "mp"),
            P("mp", "dp"),
            P(("groups", "dp", "seq"), None, "mp"),
            P("mp"),
            P(("groups", "dp", "seq")),
            P(("groups", "dp"), "mp"),
            P(("groups", "dp")),
            P(("groups", "dp"), None),
            P(("groups", "dp"), None),
        ),
        out_specs=(
            P(("groups", "dp", "seq"), None, "mp"),
            P(("groups", "dp"), None),
            P(("groups", "dp")),
        ),
        check_vma=False,
    )
```

```python
import functools

import jax
import jax.numpy as jnp
from jax import lax
from jax.experimental import pallas as pl
from jax.experimental.pallas import tpu as pltpu
from jax.sharding import PartitionSpec as P

D = 4096


epsilon = 1e-05
safety_margin = 1e-06
sharpness_divisor = 0.05
teacher_scale = 8.0


def partition_logarithm(value_rows):
    return jnp.log(jnp.sum(jnp.exp(value_rows), axis=-1, keepdims=True))


MESH = pl.DeviceIdType.MESH
CHUNKS = 14
WINDOW = 3
LAG = 2
RIGHT, LEFT, ACROSS, CORE, CORE_ACROSS = range(5)


def both(*terms):
    return functools.reduce(jnp.logical_and, terms)


def gather_kernel(w_ref, h_ref, o_ref, p_ref, t_ref, own_send, own_recv, h_send, h_recv, send, recv):
    z = lax.axis_index("dp")
    y = lax.axis_index("groups")
    c = lax.axis_index("seq")
    depth = w_ref.shape[0]
    quarter = depth // 4
    size = quarter // CHUNKS
    mine = y * 2 + c
    other = (1 - y) * 2 + c
    pair = z + 1 - 2 * (z % 2)
    to = {
        RIGHT: {"dp": jnp.minimum(z + 1, 3)},
        LEFT: {"dp": jnp.maximum(z - 1, 0)},
        ACROSS: {"groups": 1 - y},
        CORE: {"seq": 1 - c},
        CORE_ACROSS: {"seq": 1 - c},
    }

    barrier = pltpu.get_barrier_semaphore()
    pl.semaphore_signal(barrier, inc=1, device_id=to[ACROSS], device_id_type=MESH)
    pl.semaphore_signal(barrier, inc=1, device_id=to[CORE], device_id_type=MESH)

    @pl.when(z < 3)
    def _():
        pl.semaphore_signal(barrier, inc=1, device_id=to[RIGHT], device_id_type=MESH)

    @pl.when(z > 0)
    def _():
        pl.semaphore_signal(barrier, inc=1, device_id=to[LEFT], device_id_type=MESH)

    peers = 2 + (z < 3).astype(jnp.int32) + (z > 0).astype(jnp.int32)
    pl.semaphore_wait(barrier, peers)

    def rows(q, k):
        return pl.ds(pl.multiple_of(q * quarter + k * size, 16), size)

    def part(k):
        return pl.ds(pl.multiple_of(k * size, 16), size)

    def remote(kind, j, k, src, dst, arrives):
        return pltpu.make_async_remote_copy(
            src_ref=src,
            dst_ref=dst,
            send_sem=send.at[kind, j, k],
            recv_sem=recv.at[kind, arrives, k],
            device_id=to[kind],
            device_id_type=MESH,
        )

    def along(kind, j, k):
        return remote(kind, j, k, p_ref.at[part(k), :], p_ref.at[part(k), :], j)

    def shared(kind, j, k, q):
        block = jnp.where(z >= 2, z - j, z + j) % 2
        place = o_ref.at[block, rows(q, k), :]
        return remote(kind, j, k, place, place, j)

    def stream(kind, t):
        u = z if kind == RIGHT else 3 - z
        sign = -1 if kind == RIGHT else 1
        j, k = t // CHUNKS, t % CHUNKS
        own = w_ref.at[rows(mine, k), :]
        passing = p_ref.at[part(k), :]

        @pl.when(both(j == 0, u == 0))
        def _():
            remote(kind, 0, k, own, passing, 1).start()

        @pl.when(both(j == 0, u >= 1, u <= 2))
        def _():
            remote(kind, 0, k, own, o_ref.at[z % 2, rows(mine, k), :], 1).start()

        @pl.when(both(j == 1, u == 1))
        def _():
            along(kind, 1, k).wait_recv()
            place = o_ref.at[(z + sign) % 2, rows(mine, k), :]
            remote(kind, 1, k, passing, place, 2).start()

        @pl.when(jnp.logical_or(both(j == 1, u >= 2), both(j == 2, u == 2)))
        def _():
            along(kind, j, k).wait_recv()
            shared(ACROSS, j, k, mine).start()
            shared(CORE, j, k, mine).start()

        before = t - WINDOW
        jb, kb = before // CHUNKS, before % CHUNKS
        sent = jnp.logical_or(both(jb == 0, u <= 2), both(jb == 1, u == 1))

        @pl.when(both(before >= 0, sent))
        def _():
            along(kind, jb, kb).wait_send()

    def needed(j):
        return jnp.logical_or(j == 1, both(j == 2, z >= 1, z <= 2))

    swap = pltpu.make_async_remote_copy(
        src_ref=h_ref,
        dst_ref=t_ref,
        send_sem=h_send,
        recv_sem=h_recv,
        device_id={"dp": pair},
        device_id_type=MESH,
    )
    outer = jnp.logical_or(z == 0, z == 3)
    keep = pltpu.make_async_remote_copy(
        src_ref=w_ref,
        dst_ref=o_ref.at[z % 2],
        send_sem=own_send,
        recv_sem=own_recv,
        device_id=to[CORE],
        device_id_type=MESH,
    )

    def step(t, carry):
        stream(RIGHT, t)
        stream(LEFT, t)
        late = t - LAG
        j, k = late // CHUNKS, late % CHUNKS

        @pl.when(both(late >= 0, needed(j)))
        def _():
            shared(ACROSS, j, k, other).wait_recv()
            shared(CORE_ACROSS, j, k, other).start()

        @pl.when(t == CHUNKS)
        def _():
            swap.start()

            @pl.when(outer)
            def _():
                keep.start()

        return carry

    lax.fori_loop(0, 3 * CHUNKS + max(WINDOW, LAG), step, 0)

    def drain(t, carry):
        j, k = t // CHUNKS, t % CHUNKS

        @pl.when(needed(j))
        def _():
            shared(ACROSS, j, k, mine).wait_send()
            shared(CORE, j, k, mine).wait_send()
            shared(CORE, j, k, y * 2 + 1 - c).wait_recv()
            shared(CORE_ACROSS, j, k, other).wait_send()
            shared(CORE_ACROSS, j, k, (1 - y) * 2 + 1 - c).wait_recv()

        return carry

    lax.fori_loop(CHUNKS, 3 * CHUNKS, drain, 0)
    swap.wait()

    @pl.when(outer)
    def _():
        keep.wait()


def gather(weight, rows):
    depth, cols = weight.shape
    return pl.pallas_call(
        gather_kernel,
        out_shape=(
            jax.ShapeDtypeStruct((2, depth, cols), weight.dtype),
            jax.ShapeDtypeStruct((depth // 4, cols), weight.dtype),
            jax.ShapeDtypeStruct(rows.shape, rows.dtype),
        ),
        in_specs=[pl.BlockSpec(memory_space=pl.ANY)] * 2,
        out_specs=(pl.BlockSpec(memory_space=pl.ANY),) * 3,
        scratch_shapes=[
            pltpu.SemaphoreType.DMA,
            pltpu.SemaphoreType.DMA,
            pltpu.SemaphoreType.DMA,
            pltpu.SemaphoreType.DMA,
            pltpu.SemaphoreType.DMA((5, 3, CHUNKS)),
            pltpu.SemaphoreType.DMA((5, 3, CHUNKS)),
        ],
        compiler_params=pltpu.CompilerParams(collective_id=0, has_side_effects=True),
        cost_estimate=pl.CostEstimate(
            flops=0, bytes_accessed=16 * depth * cols, transcendentals=0
        ),
    )(weight, rows)


def paired_branch(flattened, weight):
    blocks, _, theirs = gather(weight, flattened)
    half = lax.axis_index("dp") % 2
    kept_here = half == lax.axis_index("mp")
    swap_pair = [(z, z + 1 - 2 * (z % 2)) for z in range(4)]
    sums = []
    back = []
    owns = []
    for s in range(2):
        away = jnp.dot(theirs, blocks[s], preferred_element_type=jnp.float32)
        back.append(lax.ppermute(away, "dp", swap_pair))
    for s in range(2):
        own = jnp.dot(flattened, blocks[s], preferred_element_type=jnp.float32)
        owns.append(lax.optimization_barrier(own))
    for s in range(2):
        leaves = jnp.where(kept_here, back[s], owns[s])
        stays = jnp.where(kept_here, owns[s], back[s])
        sums.append(stays + lax.ppermute(leaves, "mp", [(0, 1), (1, 0)]))
    return jnp.concatenate(sums, axis=1)


def local(
    paired,
    hidden,
    down_weight,
    residual,
    norm_gain,
    lengths,
    queries,
    positive_ids,
    negative_ids,
    rerank_scores,
):
    passages, tok_len, hidden_width = hidden.shape
    flattened = hidden.reshape(passages * tok_len, hidden_width)
    if paired:
        branch_sum = paired_branch(flattened, down_weight).reshape(residual.shape)
    else:
        partial_sum = jnp.dot(
            flattened,
            lax.all_gather(down_weight, "dp", axis=1, tiled=True),
            preferred_element_type=jnp.float32,
        )
        partial_sum = partial_sum.reshape(passages, tok_len, D)
        branch_sum = lax.psum_scatter(partial_sum, "mp", scatter_dimension=2, tiled=True)
    updated = residual.astype(jnp.float32) + branch_sum
    squares = lax.psum(jnp.sum(updated * updated, axis=-1), "mp")
    unit_rows = updated * lax.rsqrt(squares / D + epsilon)[:, :, None]
    scaled = unit_rows * norm_gain[None, None, :]
    position = jnp.arange(tok_len, dtype=jnp.int32)
    valid_mask = position[None, :] < lengths[:, None]
    pooled_share = (
        jnp.sum(jnp.where(valid_mask[:, :, None], scaled, 0.0), axis=1)
        / lengths.astype(jnp.float32)[:, None]
    )
    averaged_embedding = lax.all_gather(pooled_share, ("dp", "seq"), axis=0, tiled=True)
    total_passages = averaged_embedding.shape[0]
    candidates = jnp.concatenate([positive_ids[:, None], negative_ids], axis=1)
    one_hot = (
        candidates[:, :, None] == jnp.arange(total_passages, dtype=jnp.int32)[None, None, :]
    ).astype(jnp.float32)
    picked = jnp.einsum("qcp,pd->qcd", one_hot, averaged_embedding, precision=lax.Precision.HIGHEST)
    query_vals = queries.astype(jnp.float32)
    cosine_numerator = jnp.einsum("qd,qcd->qc", query_vals, picked, precision=lax.Precision.HIGHEST)
    candidate_length_power = jnp.sum(picked * picked, axis=-1)
    question_length_power = jnp.sum(query_vals * query_vals, axis=-1)
    cosine_numerator, candidate_length_power, question_length_power = lax.psum(
        (cosine_numerator, candidate_length_power, question_length_power), "mp"
    )
    similarity_matrix = (
        cosine_numerator
        * lax.rsqrt(question_length_power + safety_margin)[:, None]
        * lax.rsqrt(candidate_length_power + safety_margin)
        / sharpness_divisor
    )
    log_student = similarity_matrix - partition_logarithm(similarity_matrix)
    teacher = rerank_scores.astype(jnp.float32) / teacher_scale
    teacher_log_probs = teacher - partition_logarithm(teacher)
    losses = -log_student[:, 0] + jnp.sum(
        jnp.exp(teacher_log_probs) * (teacher_log_probs - log_student), axis=-1
    )
    return (scaled.astype(jnp.bfloat16), similarity_matrix, losses)


def solution(mesh):
    paired = (mesh.shape["dp"], mesh.shape["mp"]) == (4, 2)
    paired = paired and (mesh.shape["groups"], mesh.shape["seq"]) == (2, 2)
    return jax.shard_map(
        functools.partial(local, paired),
        mesh=mesh,
        in_specs=(
            P(("groups", "dp", "seq"), None, "mp"),
            P("mp", "dp"),
            P(("groups", "dp", "seq"), None, "mp"),
            P("mp"),
            P(("groups", "dp", "seq")),
            P(("groups", "dp"), "mp"),
            P(("groups", "dp")),
            P(("groups", "dp"), None),
            P(("groups", "dp"), None),
        ),
        out_specs=(
            P(("groups", "dp", "seq"), None, "mp"),
            P(("groups", "dp"), None),
            P(("groups", "dp")),
        ),
        check_vma=False,
    )
```

```python
import functools

import jax
import jax.numpy as jnp
from jax import lax
from jax.experimental import pallas as pl
from jax.experimental.pallas import tpu as pltpu
from jax.sharding import PartitionSpec as P

D = 4096


epsilon = 1e-05
safety_margin = 1e-06
sharpness_divisor = 0.05
teacher_scale = 8.0


def partition_logarithm(value_rows):
    return jnp.log(jnp.sum(jnp.exp(value_rows), axis=-1, keepdims=True))


MESH = pl.DeviceIdType.MESH
CHUNKS = 14
WINDOW = 3
LAG = 2
RIGHT, LEFT, ACROSS, CORE, CORE_ACROSS = range(5)


def both(*terms):
    return functools.reduce(jnp.logical_and, terms)


def gather_kernel(w_ref, h_ref, o_ref, p_ref, t_ref, own_send, own_recv, h_send, h_recv, send, recv):
    z = lax.axis_index("dp")
    y = lax.axis_index("groups")
    c = lax.axis_index("seq")
    depth = w_ref.shape[0]
    quarter = depth // 4
    size = quarter // CHUNKS
    mine = y * 2 + c
    other = (1 - y) * 2 + c
    pair = z + 1 - 2 * (z % 2)
    to = {
        RIGHT: {"dp": jnp.minimum(z + 1, 3)},
        LEFT: {"dp": jnp.maximum(z - 1, 0)},
        ACROSS: {"groups": 1 - y},
        CORE: {"seq": 1 - c},
        CORE_ACROSS: {"seq": 1 - c},
    }

    barrier = pltpu.get_barrier_semaphore()
    pl.semaphore_signal(barrier, inc=1, device_id=to[ACROSS], device_id_type=MESH)
    pl.semaphore_signal(barrier, inc=1, device_id=to[CORE], device_id_type=MESH)

    @pl.when(z < 3)
    def _():
        pl.semaphore_signal(barrier, inc=1, device_id=to[RIGHT], device_id_type=MESH)

    @pl.when(z > 0)
    def _():
        pl.semaphore_signal(barrier, inc=1, device_id=to[LEFT], device_id_type=MESH)

    peers = 2 + (z < 3).astype(jnp.int32) + (z > 0).astype(jnp.int32)
    pl.semaphore_wait(barrier, peers)

    def rows(q, k):
        return pl.ds(pl.multiple_of(q * quarter + k * size, 16), size)

    def part(k):
        return pl.ds(pl.multiple_of(k * size, 16), size)

    def remote(kind, j, k, src, dst, arrives):
        return pltpu.make_async_remote_copy(
            src_ref=src,
            dst_ref=dst,
            send_sem=send.at[kind, j, k],
            recv_sem=recv.at[kind, arrives, k],
            device_id=to[kind],
            device_id_type=MESH,
        )

    def along(kind, j, k):
        return remote(kind, j, k, p_ref.at[part(k), :], p_ref.at[part(k), :], j)

    def shared(kind, j, k, q):
        block = jnp.where(z >= 2, z - j, z + j) % 2
        place = o_ref.at[block, rows(q, k), :]
        return remote(kind, j, k, place, place, j)

    def stream(kind, t):
        u = z if kind == RIGHT else 3 - z
        sign = -1 if kind == RIGHT else 1
        j, k = t // CHUNKS, t % CHUNKS
        own = w_ref.at[rows(mine, k), :]
        passing = p_ref.at[part(k), :]

        @pl.when(both(j == 0, u == 0))
        def _():
            remote(kind, 0, k, own, passing, 1).start()

        @pl.when(both(j == 0, u >= 1, u <= 2))
        def _():
            remote(kind, 0, k, own, o_ref.at[z % 2, rows(mine, k), :], 1).start()

        @pl.when(both(j == 1, u == 1))
        def _():
            along(kind, 1, k).wait_recv()
            place = o_ref.at[(z + sign) % 2, rows(mine, k), :]
            remote(kind, 1, k, passing, place, 2).start()

        @pl.when(jnp.logical_or(both(j == 1, u >= 2), both(j == 2, u == 2)))
        def _():
            along(kind, j, k).wait_recv()
            shared(ACROSS, j, k, mine).start()
            shared(CORE, j, k, mine).start()

        before = t - WINDOW
        jb, kb = before // CHUNKS, before % CHUNKS
        sent = jnp.logical_or(both(jb == 0, u <= 2), both(jb == 1, u == 1))

        @pl.when(both(before >= 0, sent))
        def _():
            along(kind, jb, kb).wait_send()

    def needed(j):
        return jnp.logical_or(j == 1, both(j == 2, z >= 1, z <= 2))

    swap = pltpu.make_async_remote_copy(
        src_ref=h_ref,
        dst_ref=t_ref,
        send_sem=h_send,
        recv_sem=h_recv,
        device_id={"dp": pair},
        device_id_type=MESH,
    )
    outer = jnp.logical_or(z == 0, z == 3)
    keep = pltpu.make_async_remote_copy(
        src_ref=w_ref,
        dst_ref=o_ref.at[z % 2],
        send_sem=own_send,
        recv_sem=own_recv,
        device_id=to[CORE],
        device_id_type=MESH,
    )

    def step(t, carry):
        stream(RIGHT, t)
        stream(LEFT, t)
        late = t - LAG
        j, k = late // CHUNKS, late % CHUNKS

        @pl.when(both(late >= 0, needed(j)))
        def _():
            shared(ACROSS, j, k, other).wait_recv()
            shared(CORE_ACROSS, j, k, other).start()

        @pl.when(t == CHUNKS)
        def _():
            swap.start()

            @pl.when(outer)
            def _():
                keep.start()

        return carry

    lax.fori_loop(0, 3 * CHUNKS + max(WINDOW, LAG), step, 0)

    def drain(t, carry):
        j, k = t // CHUNKS, t % CHUNKS

        @pl.when(needed(j))
        def _():
            shared(ACROSS, j, k, mine).wait_send()
            shared(CORE, j, k, mine).wait_send()
            shared(CORE, j, k, y * 2 + 1 - c).wait_recv()
            shared(CORE_ACROSS, j, k, other).wait_send()
            shared(CORE_ACROSS, j, k, (1 - y) * 2 + 1 - c).wait_recv()

        return carry

    lax.fori_loop(CHUNKS, 3 * CHUNKS, drain, 0)
    swap.wait()

    @pl.when(outer)
    def _():
        keep.wait()


def gather(weight, rows):
    depth, cols = weight.shape
    return pl.pallas_call(
        gather_kernel,
        out_shape=(
            jax.ShapeDtypeStruct((2, depth, cols), weight.dtype),
            jax.ShapeDtypeStruct((depth // 4, cols), weight.dtype),
            jax.ShapeDtypeStruct(rows.shape, rows.dtype),
        ),
        in_specs=[pl.BlockSpec(memory_space=pl.ANY)] * 2,
        out_specs=(pl.BlockSpec(memory_space=pl.ANY),) * 3,
        scratch_shapes=[
            pltpu.SemaphoreType.DMA,
            pltpu.SemaphoreType.DMA,
            pltpu.SemaphoreType.DMA,
            pltpu.SemaphoreType.DMA,
            pltpu.SemaphoreType.DMA((5, 3, CHUNKS)),
            pltpu.SemaphoreType.DMA((5, 3, CHUNKS)),
        ],
        compiler_params=pltpu.CompilerParams(collective_id=0, has_side_effects=True),
        cost_estimate=pl.CostEstimate(
            flops=0, bytes_accessed=16 * depth * cols, transcendentals=0
        ),
    )(weight, rows)


def paired_branch(flattened, weight):
    blocks, _, theirs = gather(weight, flattened)
    half = lax.axis_index("dp") % 2
    kept_here = half == lax.axis_index("mp")
    swap_pair = [(z, z + 1 - 2 * (z % 2)) for z in range(4)]
    sums = []
    back = []
    owns = []
    for s in range(2):
        away = jnp.dot(theirs, blocks[s], preferred_element_type=jnp.float32)
        for piece in jnp.split(away, 2, axis=1):
            back.append(lax.ppermute(piece, "dp", swap_pair))
    for s in range(2):
        own = jnp.dot(flattened, blocks[s], preferred_element_type=jnp.float32)
        owns.extend(jnp.split(lax.optimization_barrier(own), 2, axis=1))
    for s in range(4):
        leaves = jnp.where(kept_here, back[s], owns[s])
        stays = jnp.where(kept_here, owns[s], back[s])
        sums.append(stays + lax.ppermute(leaves, "mp", [(0, 1), (1, 0)]))
    return jnp.concatenate(sums, axis=1)


def local(
    paired,
    hidden,
    down_weight,
    residual,
    norm_gain,
    lengths,
    queries,
    positive_ids,
    negative_ids,
    rerank_scores,
):
    passages, tok_len, hidden_width = hidden.shape
    flattened = hidden.reshape(passages * tok_len, hidden_width)
    if paired:
        branch_sum = paired_branch(flattened, down_weight).reshape(residual.shape)
    else:
        partial_sum = jnp.dot(
            flattened,
            lax.all_gather(down_weight, "dp", axis=1, tiled=True),
            preferred_element_type=jnp.float32,
        )
        partial_sum = partial_sum.reshape(passages, tok_len, D)
        branch_sum = lax.psum_scatter(partial_sum, "mp", scatter_dimension=2, tiled=True)
    updated = residual.astype(jnp.float32) + branch_sum
    squares = lax.psum(jnp.sum(updated * updated, axis=-1), "mp")
    unit_rows = updated * lax.rsqrt(squares / D + epsilon)[:, :, None]
    scaled = unit_rows * norm_gain[None, None, :]
    position = jnp.arange(tok_len, dtype=jnp.int32)
    valid_mask = position[None, :] < lengths[:, None]
    pooled_share = (
        jnp.sum(jnp.where(valid_mask[:, :, None], scaled, 0.0), axis=1)
        / lengths.astype(jnp.float32)[:, None]
    )
    averaged_embedding = lax.all_gather(pooled_share, ("dp", "seq"), axis=0, tiled=True)
    total_passages = averaged_embedding.shape[0]
    candidates = jnp.concatenate([positive_ids[:, None], negative_ids], axis=1)
    one_hot = (
        candidates[:, :, None] == jnp.arange(total_passages, dtype=jnp.int32)[None, None, :]
    ).astype(jnp.float32)
    picked = jnp.einsum("qcp,pd->qcd", one_hot, averaged_embedding, precision=lax.Precision.HIGHEST)
    query_vals = queries.astype(jnp.float32)
    cosine_numerator = jnp.einsum("qd,qcd->qc", query_vals, picked, precision=lax.Precision.HIGHEST)
    candidate_length_power = jnp.sum(picked * picked, axis=-1)
    question_length_power = jnp.sum(query_vals * query_vals, axis=-1)
    cosine_numerator, candidate_length_power, question_length_power = lax.psum(
        (cosine_numerator, candidate_length_power, question_length_power), "mp"
    )
    similarity_matrix = (
        cosine_numerator
        * lax.rsqrt(question_length_power + safety_margin)[:, None]
        * lax.rsqrt(candidate_length_power + safety_margin)
        / sharpness_divisor
    )
    log_student = similarity_matrix - partition_logarithm(similarity_matrix)
    teacher = rerank_scores.astype(jnp.float32) / teacher_scale
    teacher_log_probs = teacher - partition_logarithm(teacher)
    losses = -log_student[:, 0] + jnp.sum(
        jnp.exp(teacher_log_probs) * (teacher_log_probs - log_student), axis=-1
    )
    return (scaled.astype(jnp.bfloat16), similarity_matrix, losses)


def solution(mesh):
    paired = (mesh.shape["dp"], mesh.shape["mp"]) == (4, 2)
    paired = paired and (mesh.shape["groups"], mesh.shape["seq"]) == (2, 2)
    return jax.shard_map(
        functools.partial(local, paired),
        mesh=mesh,
        in_specs=(
            P(("groups", "dp", "seq"), None, "mp"),
            P("mp", "dp"),
            P(("groups", "dp", "seq"), None, "mp"),
            P("mp"),
            P(("groups", "dp", "seq")),
            P(("groups", "dp"), "mp"),
            P(("groups", "dp")),
            P(("groups", "dp"), None),
            P(("groups", "dp"), None),
        ),
        out_specs=(
            P(("groups", "dp", "seq"), None, "mp"),
            P(("groups", "dp"), None),
            P(("groups", "dp")),
        ),
        check_vma=False,
    )
```
